32 devices in a mesh: seq: 8 (over y, x, core), head: 4 (over z).
Axes of the slice: x: 2, y: 2, z: 4, core: 2. Of those that a mesh axis runs over, the one named last changes fastest.
Arguments:
- queries: bfloat16 [4096, 8192], P(('seq', 'head')), may hold values from -18 to 18
- keys: bfloat16 [4096, 1024], P(('seq', 'head')), may hold values from -18 to 18
- values: bfloat16 [4096, 1024], P(('seq', 'head')), may hold values from -6 to 6
- grad_out: bfloat16 [4096, 8192], P(('seq', 'head')), may hold values from -6 to 6
- starts: int32 [8], replicated, may hold values from 0 to 4095, as said below
- pattern: int32 [32, 5], replicated, may hold values from 0 to 1, as said below
Outputs:
- query_grads: bfloat16 [4096, 8192], P(('seq', 'head'))
- key_grads: bfloat16 [4096, 1024], P(('seq', 'head'))
- value_grads: bfloat16 [4096, 1024], P(('seq', 'head'))
The draws below stay inside these ranges and needn't reach their ends.
Inputs may be any that keep to these rules, and one draw needn't show every extreme that they name: starts[0] is 0, the offsets rise strictly and the last is 4095; sequence i runs from starts[i] to the next offset (the last to the end). `pattern`: column 0 is all ones.
All inputs are finite; a program needn't handle non-finite values.
Results may differ from the reference program's by a relative error of at most 0.0074.
Values may be sent and summed in bfloat16 or wider, within the bound.
A program may use at most 192 MiB of HBM per device.

```python
import math
import jax
import jax.numpy as jnp
from jax import lax

HEADS = 64
KV_HEADS = 8
HEAD_DIM = 128
WINDOW = 512
BLOCK = 128
TOKENS = 4096
NSEQ = 8
NBLK = 32


def paired_draw(key):
    kv_noise = jnp.clip(jax.random.normal(jax.random.fold_in(key, 11), (TOKENS, KV_HEADS, HEAD_DIM), jnp.float32), -4.0, 4.0)
    query_noise = jnp.clip(jax.random.normal(jax.random.fold_in(key, 12), (TOKENS, HEADS, HEAD_DIM), jnp.float32), -4.0, 4.0)
    queries_out = query_noise
    keys_out = kv_noise
    return (queries_out.reshape(TOKENS, -1), keys_out.reshape(TOKENS, -1))


def draw_queries(key, part):
    return paired_draw(key)[0].astype(jnp.bfloat16)


def draw_keys(key, part):
    return paired_draw(key)[1].astype(jnp.bfloat16)


def draw_starts(key, part):
    picks = jax.random.permutation(jax.random.fold_in(key, 21), TOKENS - 2)[:NSEQ - 2] + 1
    inner = jnp.sort(picks).astype(jnp.int32)
    return jnp.concatenate([jnp.zeros((1,), jnp.int32), inner, jnp.full((1,), TOKENS - 1, jnp.int32)])


def draw_pattern(key, part):
    coins = jax.random.randint(jax.random.fold_in(key, 31), (NBLK, WINDOW // BLOCK + 1), 0, 4)
    opened = (coins > 0).astype(jnp.int32)
    return opened.at[:, 0].set(1)


def level_of(stream_key, dims, pieces, smallest, largest):
    factor_of, own = 1.0, jax.random.fold_in(stream_key, 6)
    for dim, shards_of in pieces:
        draws = jnp.exp(jax.random.uniform(jax.random.fold_in(own, dim), (shards_of,), jnp.float32, smallest / len(pieces), largest / len(pieces)))
        factor_of = factor_of * jnp.repeat(draws, dims[dim] // shards_of).reshape([-1 if axis == dim else 1 for axis in range(len(dims))])
    return factor_of


def centred(key, dims, spread, bound, cuts=(), held_as=jnp.bfloat16):
    drawn = spread * jax.random.normal(key, dims, jnp.float32)
    if cuts:
        drawn = drawn * level_of(key, dims, cuts, -0.22, 0.18)
    return jnp.clip(drawn, -bound, bound).astype(held_as)


def setup_inputs(seed: int = 0) -> dict:
    streams_of = jax.random.split(jax.random.key(seed), 7)
    queries = draw_queries(jax.random.fold_in(streams_of[6], 71), 0)
    keys = draw_keys(jax.random.fold_in(streams_of[6], 71), 0)
    values = centred(streams_of[2], (TOKENS, KV_HEADS * HEAD_DIM), 1.0, 6.0, ((0, 32),))
    grad_out = centred(streams_of[3], (TOKENS, HEADS * HEAD_DIM), 1.0, 6.0, ((0, 32),))
    starts = draw_starts(jax.random.fold_in(streams_of[6], 71), 0)
    pattern = draw_pattern(jax.random.fold_in(streams_of[6], 71), 0)
    return {"queries": queries, "keys": keys, "values": values, "grad_out": grad_out, "starts": starts, "pattern": pattern}


def segment_of(positions, starts):
    return lax.optimization_barrier(jnp.sum((starts[None, :] <= positions[:, None]).astype(jnp.int32), axis=1)) - 1

def block_allowed(first_row, starts, pattern):
    query_pos = first_row + jnp.arange(WINDOW, dtype=jnp.int32)
    key_pos = first_row - WINDOW + jnp.arange(2 * WINDOW, dtype=jnp.int32)
    per_block = WINDOW // BLOCK
    pattern_rows = lax.dynamic_slice(pattern, ((first_row // BLOCK).astype(jnp.int32), jnp.zeros((), jnp.int32)), (per_block, per_block + 1))
    relative = jnp.arange(per_block, dtype=jnp.int32)[:, None] - jnp.arange(2 * per_block, dtype=jnp.int32)[None, :] + per_block
    matches = (jnp.arange(per_block + 1, dtype=jnp.int32)[None, None, :] == relative[:, :, None]).astype(jnp.int32)
    chosen = lax.optimization_barrier(jnp.sum(pattern_rows[:, None, :] * matches, axis=2))
    block_open = jnp.repeat(jnp.repeat(chosen, BLOCK, axis=0), BLOCK, axis=1) > 0
    query_col = query_pos[:, None]
    key_row = key_pos[None, :]
    same_seq = segment_of(query_pos, starts)[:, None] == segment_of(key_pos, starts)[None, :]
    return (key_row <= query_col) & (query_col - key_row < WINDOW) & (key_row >= 0) & same_seq & block_open

def block_grads(query_blk, key_blk, value_blk, grad_blk, allowed, kv_local, head_dim):
    count_rows = query_blk.shape[0]
    count_keys = key_blk.shape[0]
    query_heads = query_blk.astype(jnp.float32).reshape(count_rows, kv_local, -1, head_dim)
    grad_heads = grad_blk.astype(jnp.float32).reshape(count_rows, kv_local, -1, head_dim)
    key_heads = key_blk.astype(jnp.float32).reshape(count_keys, kv_local, head_dim)
    value_heads = value_blk.astype(jnp.float32).reshape(count_keys, kv_local, head_dim)
    score_scale = 1.0 / math.sqrt(head_dim)
    score = score_scale * jnp.einsum('rkgd,nkd->kgrn', query_heads, key_heads)
    mask = allowed[None, None]
    peak = lax.optimization_barrier(jnp.max(jnp.where(mask, score, -1e+30), axis=-1, keepdims=True))
    expo = jnp.exp(jnp.where(mask, score - peak, -1e+30))
    probs = expo / lax.optimization_barrier(jnp.sum(expo, axis=-1, keepdims=True))
    probs_low = probs.astype(jnp.bfloat16)
    value_grad = jnp.einsum('kgrn,rkgd->nkd', probs_low.astype(jnp.float32), grad_heads)
    prob_grad = jnp.einsum('rkgd,nkd->kgrn', grad_heads, value_heads)
    row_dot = lax.optimization_barrier(jnp.sum(probs * prob_grad, axis=-1, keepdims=True))
    score_grad = (probs * (prob_grad - row_dot)).astype(jnp.bfloat16).astype(jnp.float32)
    query_grad = score_scale * jnp.einsum('kgrn,nkd->rkgd', score_grad, key_heads)
    key_grad = score_scale * jnp.einsum('kgrn,rkgd->nkd', score_grad, query_heads)
    return (query_grad.reshape(count_rows, -1), key_grad.reshape(count_keys, -1), value_grad.reshape(count_keys, -1))

def reference(queries, keys, values, grad_out, starts, pattern):
    count_tokens = queries.shape[0]
    kv_width = keys.shape[1]
    key_pad = jnp.concatenate([jnp.zeros((WINDOW, kv_width), keys.dtype), keys], axis=0)
    value_pad = jnp.concatenate([jnp.zeros((WINDOW, kv_width), values.dtype), values], axis=0)

    def step(carry, block_index):
        key_acc, value_acc = carry
        first_row = (block_index * WINDOW).astype(jnp.int32)
        allowed = block_allowed(first_row, starts, pattern)
        query_blk = lax.dynamic_slice_in_dim(queries, first_row, WINDOW, 0)
        grad_blk = lax.dynamic_slice_in_dim(grad_out, first_row, WINDOW, 0)
        key_blk = lax.dynamic_slice_in_dim(key_pad, first_row, 2 * WINDOW, 0)
        value_blk = lax.dynamic_slice_in_dim(value_pad, first_row, 2 * WINDOW, 0)
        query_grad, key_grad, value_grad = block_grads(query_blk, key_blk, value_blk, grad_blk, allowed, KV_HEADS, HEAD_DIM)
        key_acc = lax.dynamic_update_slice_in_dim(key_acc, lax.dynamic_slice_in_dim(key_acc, first_row, 2 * WINDOW, 0) + key_grad, first_row, 0)
        value_acc = lax.dynamic_update_slice_in_dim(value_acc, lax.dynamic_slice_in_dim(value_acc, first_row, 2 * WINDOW, 0) + value_grad, first_row, 0)
        return ((key_acc, value_acc), query_grad.astype(jnp.bfloat16))
    empty = jnp.zeros((WINDOW + count_tokens, kv_width), jnp.float32)
    (key_acc, value_acc), query_parts = lax.scan(step, (empty, empty), jnp.arange(count_tokens // WINDOW, dtype=jnp.int32))
    query_grads = query_parts.reshape(count_tokens, -1)
    return (query_grads, key_acc[WINDOW:].astype(jnp.bfloat16), value_acc[WINDOW:].astype(jnp.bfloat16))
```

```python
import functools
import math

import jax
import jax.numpy as jnp
from jax import lax
from jax.experimental import pallas as pl
from jax.experimental.pallas import tpu as pltpu
from jax.sharding import PartitionSpec as P

KV_HEADS = 8
HEAD_DIM = 128
WINDOW = 512
BLOCK = 128
BACK = WINDOW // BLOCK
AXES = ("seq", "head")
GROUPS = 2

SCALE = 1.0 / math.sqrt(HEAD_DIM)


def mask_bias(first_row, starts_ref, pattern_ref, block):
    shape = ((BACK + 1) * BLOCK, BLOCK)
    row = lax.broadcasted_iota(jnp.int32, shape, 0)
    query_pos = first_row + lax.broadcasted_iota(jnp.int32, shape, 1)
    back = row // BLOCK
    key_pos = first_row - back * BLOCK + (row - back * BLOCK)
    crossed = jnp.zeros(shape, jnp.int32)
    for i in range(starts_ref.shape[0]):
        start = starts_ref[i]
        crossed += ((start <= query_pos) & (start > key_pos)).astype(jnp.int32)
    opened = jnp.zeros(shape, jnp.int32)
    for r in range(BACK + 1):
        opened += jnp.where(back == r, pattern_ref[block, r], 0)
    allowed = (
        (key_pos <= query_pos)
        & (query_pos - key_pos < WINDOW)
        & (key_pos >= 0)
        & (crossed == 0)
        & (opened > 0)
    )
    return jnp.where(allowed, 0.0, -1e30).astype(jnp.float32)


def dot(a, b, dims):
    return lax.dot_general(a, b, (dims, ((), ())), preferred_element_type=jnp.float32)


def head_terms(query_ref, grad_ref, query_grad_ref, first_col, group, key, value, bias):
    key_grad = None
    value_grad = None
    bias = jnp.concatenate([bias, bias], axis=1)
    for pair in range(group // 2):
        cols = [pl.ds(first_col + (2 * pair + i) * HEAD_DIM, HEAD_DIM) for i in range(2)]
        query = jnp.concatenate([query_ref[:, c] for c in cols], axis=0)
        grad = jnp.concatenate([grad_ref[:, c] for c in cols], axis=0)
        score = dot(key, query, ((1,), (1,))) * (SCALE * math.log2(math.e)) + bias
        expo = jnp.exp2(score - jnp.max(score, axis=0, keepdims=True))
        probs = expo * (1.0 / jnp.sum(expo, axis=0, keepdims=True))
        probs_low = probs.astype(jnp.bfloat16)
        prob_grad = dot(value, grad, ((1,), (1,)))
        row_dot = jnp.sum(probs * prob_grad, axis=0, keepdims=True)
        score_grad = (probs * (prob_grad - row_dot)).astype(jnp.bfloat16)
        value_part = dot(probs_low, grad, ((1,), (0,)))
        key_part = dot(score_grad, query, ((1,), (0,)))
        value_grad = value_part if value_grad is None else value_grad + value_part
        key_grad = key_part if key_grad is None else key_grad + key_part
        query_grad = (dot(score_grad, key, ((0,), (0,))) * SCALE).astype(jnp.bfloat16)
        for i in range(2):
            query_grad_ref[:, cols[i]] = query_grad[i * BLOCK : (i + 1) * BLOCK]
    return key_grad * SCALE, value_grad


def kernel(group, starts_ref, pattern_ref, query_ref, grad_ref, *refs):
    kv_refs, (query_grad_ref, own_ref, sent_ref, bias_ref) = refs[: BACK + 1], refs[BACK + 1 :]
    block = lax.axis_index("seq") * lax.axis_size("head") + lax.axis_index("head")

    @pl.when(pl.program_id(0) == 0)
    def _():
        bias_ref[...] = mask_bias(block * BLOCK, starts_ref, pattern_ref, block)

    key = jnp.concatenate([ref[0] for ref in kv_refs], axis=0)
    value = jnp.concatenate([ref[1] for ref in kv_refs], axis=0)
    key_grad, value_grad = head_terms(
        query_ref, grad_ref, query_grad_ref, 0, group, key, value, bias_ref[...]
    )
    for i, full in enumerate((key_grad, value_grad)):
        own_ref[i] = full[:BLOCK]
        for r in range(BACK):
            sent_ref[r, i] = full[(r + 1) * BLOCK : (r + 2) * BLOCK].astype(jnp.bfloat16)


def local_grads(part, heads, group, starts, pattern, queries, grad_out, kvs):
    width = group * HEAD_DIM
    wide = pl.BlockSpec((BLOCK, width), lambda h: (0, part * heads + h))
    kv_spec = pl.BlockSpec((2, BLOCK, HEAD_DIM), lambda h: (0, 0, h))
    kv_width = heads * HEAD_DIM
    smem = pl.BlockSpec(memory_space=pltpu.SMEM)
    return pl.pallas_call(
        functools.partial(kernel, group),
        grid=(heads,),
        in_specs=[smem, smem, wide, wide] + [kv_spec] * (BACK + 1),
        out_specs=[
            pl.BlockSpec((BLOCK, width), lambda h: (0, h)),
            kv_spec,
            pl.BlockSpec((BACK, 2, BLOCK, HEAD_DIM), lambda h: (0, 0, 0, h)),
        ],
        out_shape=[
            jax.ShapeDtypeStruct((BLOCK, heads * width), jnp.bfloat16),
            jax.ShapeDtypeStruct((2, BLOCK, kv_width), jnp.float32),
            jax.ShapeDtypeStruct((BACK, 2, BLOCK, kv_width), jnp.bfloat16),
        ],
        scratch_shapes=[pltpu.VMEM(((BACK + 1) * BLOCK, BLOCK), jnp.float32)],
        compiler_params=pltpu.CompilerParams(vmem_limit_bytes=40 * 2**20),
        cost_estimate=pl.CostEstimate(
            flops=heads * group * BLOCK * (BACK + 1) * BLOCK * HEAD_DIM * 40,
            bytes_accessed=heads * width * BLOCK * 6,
            transcendentals=0,
        ),
    )(starts, pattern, queries, grad_out, *kvs)


def body(queries, keys, values, grad_out, starts, pattern):
    devices = lax.axis_size("seq") * lax.axis_size("head")
    group = queries.shape[1] // keys.shape[1]
    heads = KV_HEADS // GROUPS
    kv_width = heads * HEAD_DIM
    received = []
    for part in range(GROUPS):
        cols = slice(part * kv_width, (part + 1) * kv_width)
        own = jnp.stack([keys[:, cols], values[:, cols]])
        received.append(
            [own]
            + [
                lax.ppermute(own, AXES, [(i, i + r) for i in range(devices - r)])
                for r in range(1, BACK + 1)
            ]
        )
    query_parts, kv_parts = [], []
    for part in range(GROUPS):
        query_grads, total, sent = local_grads(
            part, heads, group, starts, pattern, queries, grad_out, received[part]
        )
        query_parts.append(query_grads)
        for r in range(1, BACK + 1):
            back = lax.ppermute(sent[r - 1], AXES, [(i + r, i) for i in range(devices - r)])
            total = total + back.astype(jnp.float32)
        kv_parts.append(total.astype(jnp.bfloat16))
    both = jnp.concatenate(kv_parts, axis=2)
    return jnp.concatenate(query_parts, axis=1), both[0], both[1]


def solution(mesh):
    rows = P(AXES, None)
    return jax.shard_map(
        body,
        mesh=mesh,
        in_specs=(rows, rows, rows, rows, P(), P()),
        out_specs=(rows, rows, rows),
        check_vma=False,
    )
```

```python
import functools
import math

import jax
import jax.numpy as jnp
from jax import lax
from jax.experimental import pallas as pl
from jax.experimental.pallas import tpu as pltpu
from jax.sharding import PartitionSpec as P

KV_HEADS = 8
HEAD_DIM = 128
WINDOW = 512
BLOCK = 128
BACK = WINDOW // BLOCK
AXES = ("seq", "head")

SCALE = 1.0 / math.sqrt(HEAD_DIM)


def mask_bias(first_row, starts_ref, pattern_ref, block):
    shape = ((BACK + 1) * BLOCK, BLOCK)
    row = lax.broadcasted_iota(jnp.int32, shape, 0)
    query_pos = first_row + lax.broadcasted_iota(jnp.int32, shape, 1)
    back = row // BLOCK
    key_pos = first_row - back * BLOCK + (row - back * BLOCK)
    crossed = jnp.zeros(shape, jnp.int32)
    for i in range(starts_ref.shape[0]):
        start = starts_ref[i]
        crossed += ((start <= query_pos) & (start > key_pos)).astype(jnp.int32)
    opened = jnp.zeros(shape, jnp.int32)
    for r in range(BACK + 1):
        opened += jnp.where(back == r, pattern_ref[block, r], 0)
    allowed = (
        (key_pos <= query_pos)
        & (query_pos - key_pos < WINDOW)
        & (key_pos >= 0)
        & (crossed == 0)
        & (opened > 0)
    )
    return jnp.where(allowed, 0.0, -1e30).astype(jnp.float32)


def dot(a, b, dims):
    return lax.dot_general(a, b, (dims, ((), ())), preferred_element_type=jnp.float32)


def head_terms(query_ref, grad_ref, query_grad_ref, first_col, group, key, value, bias):
    key_grad = None
    value_grad = None
    bias = jnp.concatenate([bias, bias], axis=1)
    for pair in range(group // 2):
        cols = [
            pl.ds(pl.multiple_of(first_col + (2 * pair + i) * HEAD_DIM, HEAD_DIM), HEAD_DIM)
            for i in range(2)
        ]
        query = jnp.concatenate([query_ref[:, c] for c in cols], axis=0)
        grad = jnp.concatenate([grad_ref[:, c] for c in cols], axis=0)
        score = dot(key, query, ((1,), (1,))) * (SCALE * math.log2(math.e)) + bias
        expo = jnp.exp2(score - jnp.max(score, axis=0, keepdims=True))
        probs = expo * (1.0 / jnp.sum(expo, axis=0, keepdims=True))
        probs_low = probs.astype(jnp.bfloat16)
        prob_grad = dot(value, grad, ((1,), (1,)))
        row_dot = jnp.sum(probs * prob_grad, axis=0, keepdims=True)
        score_grad = (probs * (prob_grad - row_dot)).astype(jnp.bfloat16)
        value_part = dot(probs_low, grad, ((1,), (0,)))
        key_part = dot(score_grad, query, ((1,), (0,)))
        value_grad = value_part if value_grad is None else value_grad + value_part
        key_grad = key_part if key_grad is None else key_grad + key_part
        query_grad = (dot(score_grad, key, ((0,), (0,))) * SCALE).astype(jnp.bfloat16)
        for i in range(2):
            query_grad_ref[:, cols[i]] = query_grad[i * BLOCK : (i + 1) * BLOCK]
    return key_grad * SCALE, value_grad


def kernel(
    group,
    starts_ref,
    pattern_ref,
    query_ref,
    grad_ref,
    key_ref,
    value_ref,
    query_grad_ref,
    key_grad_ref,
    value_grad_ref,
    own_kv,
    kv_in,
    own_grads,
    grads_out,
    grads_in,
    bias_ref,
    kv_send,
    kv_recv,
    grads_send,
    grads_recv,
):
    span = lax.axis_size("head")
    devices = lax.axis_size("seq") * span
    block = lax.axis_index("seq") * span + lax.axis_index("head")
    backs = range(1, BACK + 1)

    def place(other):
        return (lax.div(other, span), lax.rem(other, span))

    def has_next(r):
        return block + r < devices

    def has_prior(r):
        return block >= r

    def kv_copy(h, r):
        return pltpu.make_async_remote_copy(
            src_ref=own_kv.at[h],
            dst_ref=kv_in.at[r - 1, h],
            send_sem=kv_send.at[r - 1, h],
            recv_sem=kv_recv.at[r - 1, h],
            device_id=place(lax.rem(block + r, devices)),
            device_id_type=pl.DeviceIdType.MESH,
        )

    def grads_copy(h, r):
        return pltpu.make_async_remote_copy(
            src_ref=grads_out.at[r - 1, h],
            dst_ref=grads_in.at[r - 1, h],
            send_sem=grads_send.at[r - 1, h],
            recv_sem=grads_recv.at[r - 1, h],
            device_id=place(lax.rem(block + devices - r, devices)),
            device_id_type=pl.DeviceIdType.MESH,
        )

    barrier = pltpu.get_barrier_semaphore()
    for r in backs:
        for there, step in ((has_next(r), r), (has_prior(r), devices - r)):

            @pl.when(there)
            def _():
                pl.semaphore_signal(
                    barrier,
                    inc=1,
                    device_id=place(lax.rem(block + step, devices)),
                    device_id_type=pl.DeviceIdType.MESH,
                )

    for h in range(KV_HEADS):
        own_kv[h, 0] = key_ref[:, h * HEAD_DIM : (h + 1) * HEAD_DIM]
        own_kv[h, 1] = value_ref[:, h * HEAD_DIM : (h + 1) * HEAD_DIM]
    partners = jnp.minimum(block, BACK) + jnp.minimum(devices - 1 - block, BACK)
    pl.semaphore_wait(barrier, partners)

    @pl.loop(0, KV_HEADS)
    def _(h):
        for r in backs:

            @pl.when(has_next(r))
            def _():
                kv_copy(h, r).start()

    for r in backs:

        @pl.when(jnp.logical_not(has_prior(r)))
        def _():
            kv_in[r - 1] = jnp.zeros(kv_in.shape[1:], kv_in.dtype)

        @pl.when(jnp.logical_not(has_next(r)))
        def _():
            grads_in[r - 1] = jnp.zeros(grads_in.shape[1:], grads_in.dtype)

    bias_ref[...] = mask_bias(block * BLOCK, starts_ref, pattern_ref, block)

    @pl.loop(0, KV_HEADS)
    def _(h):
        for r in backs:

            @pl.when(has_prior(r))
            def _():
                kv_copy(h, r).wait_recv()

        key, value = (
            jnp.concatenate([own_kv[h, i]] + [kv_in[r - 1, h, i] for r in backs], axis=0)
            for i in range(2)
        )
        terms = head_terms(
            query_ref,
            grad_ref,
            query_grad_ref,
            h * (group * HEAD_DIM),
            group,
            key,
            value,
            bias_ref[...],
        )
        for i in range(2):
            own_grads[h, i] = terms[i][:BLOCK]
            for r in backs:
                grads_out[r - 1, h, i] = terms[i][r * BLOCK : (r + 1) * BLOCK].astype(
                    jnp.bfloat16
                )
        for r in backs:

            @pl.when(has_prior(r))
            def _():
                grads_copy(h, r).start()

    @pl.loop(0, KV_HEADS)
    def _(h):
        for r in backs:

            @pl.when(has_next(r))
            def _():
                grads_copy(h, r).wait_recv()

        cols = pl.ds(pl.multiple_of(h * HEAD_DIM, HEAD_DIM), HEAD_DIM)
        for i, out_ref in enumerate((key_grad_ref, value_grad_ref)):
            total = own_grads[h, i]
            for r in backs:
                total += grads_in[r - 1, h, i].astype(jnp.float32)
            out_ref[:, cols] = total.astype(jnp.bfloat16)

    @pl.loop(0, KV_HEADS)
    def _(h):
        for r in backs:

            @pl.when(has_next(r))
            def _():
                kv_copy(h, r).wait_send()

            @pl.when(has_prior(r))
            def _():
                grads_copy(h, r).wait_send()


def body(queries, keys, values, grad_out, starts, pattern):
    group = queries.shape[1] // keys.shape[1]
    smem = pl.BlockSpec(memory_space=pltpu.SMEM)
    vmem = pl.BlockSpec(memory_space=pltpu.VMEM)
    pair = (KV_HEADS, 2, BLOCK, HEAD_DIM)
    sems = pltpu.SemaphoreType.DMA((BACK, KV_HEADS))
    return pl.pallas_call(
        functools.partial(kernel, group),
        in_specs=[smem, smem] + [vmem] * 4,
        out_specs=[vmem] * 3,
        out_shape=[
            jax.ShapeDtypeStruct(queries.shape, jnp.bfloat16),
            jax.ShapeDtypeStruct(keys.shape, jnp.bfloat16),
            jax.ShapeDtypeStruct(values.shape, jnp.bfloat16),
        ],
        scratch_shapes=[
            pltpu.VMEM(pair, jnp.bfloat16),
            pltpu.VMEM((BACK,) + pair, jnp.bfloat16),
            pltpu.VMEM(pair, jnp.float32),
            pltpu.VMEM((BACK,) + pair, jnp.bfloat16),
            pltpu.VMEM((BACK,) + pair, jnp.bfloat16),
            pltpu.VMEM(((BACK + 1) * BLOCK, BLOCK), jnp.float32),
            sems,
            sems,
            sems,
            sems,
        ],
        compiler_params=pltpu.CompilerParams(
            collective_id=0, has_side_effects=True, vmem_limit_bytes=48 * 2**20
        ),
    )(starts, pattern, queries, grad_out, keys, values)


def solution(mesh):
    rows = P(AXES, None)
    return jax.shard_map(
        body,
        mesh=mesh,
        in_specs=(rows, rows, rows, rows, P(), P()),
        out_specs=(rows, rows, rows),
        check_vma=False,
    )
```

```python
import functools
import math

import jax
import jax.numpy as jnp
from jax import lax
from jax.experimental import pallas as pl
from jax.experimental.pallas import tpu as pltpu
from jax.sharding import PartitionSpec as P

KV_HEADS = 8
HEAD_DIM = 128
WINDOW = 512
BLOCK = 128
BACK = WINDOW // BLOCK
AXES = ("seq", "head")
LEAD = 2

SCALE = 1.0 / math.sqrt(HEAD_DIM)


def mask_bias(first_row, starts_ref, pattern_ref, block):
    shape = ((BACK + 1) * BLOCK, BLOCK)
    row = lax.broadcasted_iota(jnp.int32, shape, 0)
    query_pos = first_row + lax.broadcasted_iota(jnp.int32, shape, 1)
    back = row // BLOCK
    key_pos = first_row - back * BLOCK + (row - back * BLOCK)
    crossed = jnp.zeros(shape, jnp.int32)
    for i in range(starts_ref.shape[0]):
        start = starts_ref[i]
        crossed += ((start <= query_pos) & (start > key_pos)).astype(jnp.int32)
    opened = jnp.zeros(shape, jnp.int32)
    for r in range(BACK + 1):
        opened += jnp.where(back == r, pattern_ref[block, r], 0)
    allowed = (
        (key_pos <= query_pos)
        & (query_pos - key_pos < WINDOW)
        & (key_pos >= 0)
        & (crossed == 0)
        & (opened > 0)
    )
    return jnp.where(allowed, 0.0, -1e30).astype(jnp.float32)


def dot(a, b, dims):
    return lax.dot_general(a, b, (dims, ((), ())), preferred_element_type=jnp.float32)


def head_terms(query_ref, grad_ref, query_grad_ref, first_col, group, key, value, bias):
    key_grad = None
    value_grad = None
    bias = jnp.concatenate([bias, bias], axis=1)
    for pair in range(group // 2):
        cols = [
            pl.ds(pl.multiple_of(first_col + (2 * pair + i) * HEAD_DIM, HEAD_DIM), HEAD_DIM)
            for i in range(2)
        ]
        query = jnp.concatenate([query_ref[:, c] for c in cols], axis=0)
        grad = jnp.concatenate([grad_ref[:, c] for c in cols], axis=0)
        score = dot(key, query, ((1,), (1,))) * (SCALE * math.log2(math.e)) + bias
        expo = jnp.exp2(score - jnp.max(score, axis=0, keepdims=True))
        probs = expo * (1.0 / jnp.sum(expo, axis=0, keepdims=True))
        probs_low = probs.astype(jnp.bfloat16)
        prob_grad = dot(value, grad, ((1,), (1,)))
        row_dot = jnp.sum(probs * prob_grad, axis=0, keepdims=True)
        score_grad = (probs * (prob_grad - row_dot)).astype(jnp.bfloat16)
        value_part = dot(probs_low, grad, ((1,), (0,)))
        key_part = dot(score_grad, query, ((1,), (0,)))
        value_grad = value_part if value_grad is None else value_grad + value_part
        key_grad = key_part if key_grad is None else key_grad + key_part
        query_grad = (dot(score_grad, key, ((0,), (0,))) * SCALE).astype(jnp.bfloat16)
        for i in range(2):
            query_grad_ref[:, cols[i]] = query_grad[i * BLOCK : (i + 1) * BLOCK]
    return key_grad * SCALE, value_grad


def kernel(
    group,
    starts_ref,
    pattern_ref,
    query_ref,
    grad_ref,
    key_ref,
    value_ref,
    query_grad_ref,
    key_grad_ref,
    value_grad_ref,
    own_kv,
    kv_in,
    own_grads,
    grads_out,
    grads_in,
    bias_ref,
    kv_send,
    kv_recv,
    relay_send,
    grads_send,
    grads_recv,
):
    span = lax.axis_size("head")
    devices = lax.axis_size("seq") * span
    block = lax.axis_index("seq") * span + lax.axis_index("head")
    backs = range(1, BACK + 1)

    def place(other):
        return (lax.div(other, span), lax.rem(other, span))

    def has_next(r):
        return block + r < devices

    def has_prior(r):
        return block >= r

    lane = lax.rem(block, BACK)
    direct = {1: lane != 3, 2: (lane == 0) | (lane == 3), 3: lane != 0, 4: lane >= 0}
    upward = lane == 2
    downward = (lane == 1) & (block >= BACK)
    relays = (
        (upward, 1, ((2, 3), (1, 2))),
        (downward, devices - 1, ((3, 2), (2, 1))),
    )
    early = {
        1: upward,
        2: upward | downward,
        3: downward,
        4: lane < 0,
    }

    def sends(r):
        return has_next(r) & direct[r]

    def waits_late(r):
        return has_prior(r) & jnp.logical_not(early[r])

    def kv_copy(h, r):
        return pltpu.make_async_remote_copy(
            src_ref=own_kv.at[h],
            dst_ref=kv_in.at[r - 1, h],
            send_sem=kv_send.at[r - 1, h],
            recv_sem=kv_recv.at[r - 1, h],
            device_id=place(lax.rem(block + r, devices)),
            device_id_type=pl.DeviceIdType.MESH,
        )

    def grads_copy(h, r):
        return pltpu.make_async_remote_copy(
            src_ref=grads_out.at[r - 1, h],
            dst_ref=grads_in.at[r - 1, h],
            send_sem=grads_send.at[r - 1, h],
            recv_sem=grads_recv.at[r - 1, h],
            device_id=place(lax.rem(block + devices - r, devices)),
            device_id_type=pl.DeviceIdType.MESH,
        )

    def relay_copy(h, k, step, here, there):
        return pltpu.make_async_remote_copy(
            src_ref=kv_in.at[here - 1, h],
            dst_ref=kv_in.at[there - 1, h],
            send_sem=relay_send.at[k, h],
            recv_sem=kv_recv.at[there - 1, h],
            device_id=place(lax.rem(block + step, devices)),
            device_id_type=pl.DeviceIdType.MESH,
        )

    def hand_on(h):
        for active, step, moves in relays:

            @pl.when(active)
            def _():
                for k, (here, there) in enumerate(moves):
                    kv_copy(h, here).wait_recv()
                    relay_copy(h, k, step, here, there).start()

    barrier = pltpu.get_barrier_semaphore()
    for r in backs:
        for there, step in ((has_next(r), r), (has_prior(r), devices - r)):

            @pl.when(there)
            def _():
                pl.semaphore_signal(
                    barrier,
                    inc=1,
                    device_id=place(lax.rem(block + step, devices)),
                    device_id_type=pl.DeviceIdType.MESH,
                )

    for h in range(KV_HEADS):
        own_kv[h, 0] = key_ref[:, h * HEAD_DIM : (h + 1) * HEAD_DIM]
        own_kv[h, 1] = value_ref[:, h * HEAD_DIM : (h + 1) * HEAD_DIM]
    partners = jnp.minimum(block, BACK) + jnp.minimum(devices - 1 - block, BACK)
    pl.semaphore_wait(barrier, partners)

    @pl.loop(0, KV_HEADS)
    def _(h):
        for r in backs:

            @pl.when(sends(r))
            def _():
                kv_copy(h, r).start()

    for r in backs:

        @pl.when(jnp.logical_not(has_prior(r)))
        def _():
            kv_in[r - 1] = jnp.zeros(kv_in.shape[1:], kv_in.dtype)

        @pl.when(jnp.logical_not(has_next(r)))
        def _():
            grads_in[r - 1] = jnp.zeros(grads_in.shape[1:], grads_in.dtype)

    bias_ref[...] = mask_bias(block * BLOCK, starts_ref, pattern_ref, block)

    for h in range(LEAD):
        hand_on(h)

    @pl.loop(0, KV_HEADS)
    def _(h):
        @pl.when(h + LEAD < KV_HEADS)
        def _():
            hand_on(h + LEAD)

        for r in backs:

            @pl.when(waits_late(r))
            def _():
                kv_copy(h, r).wait_recv()

        key, value = (
            jnp.concatenate([own_kv[h, i]] + [kv_in[r - 1, h, i] for r in backs], axis=0)
            for i in range(2)
        )
        terms = head_terms(
            query_ref,
            grad_ref,
            query_grad_ref,
            h * (group * HEAD_DIM),
            group,
            key,
            value,
            bias_ref[...],
        )
        for i in range(2):
            own_grads[h, i] = terms[i][:BLOCK]
            for r in backs:
                grads_out[r - 1, h, i] = terms[i][r * BLOCK : (r + 1) * BLOCK].astype(
                    jnp.bfloat16
                )
        for r in backs:

            @pl.when(has_prior(r))
            def _():
                grads_copy(h, r).start()

    @pl.loop(0, KV_HEADS)
    def _(h):
        for r in backs:

            @pl.when(has_next(r))
            def _():
                grads_copy(h, r).wait_recv()

        cols = pl.ds(pl.multiple_of(h * HEAD_DIM, HEAD_DIM), HEAD_DIM)
        for i, out_ref in enumerate((key_grad_ref, value_grad_ref)):
            total = own_grads[h, i]
            for r in backs:
                total += grads_in[r - 1, h, i].astype(jnp.float32)
            out_ref[:, cols] = total.astype(jnp.bfloat16)

    @pl.loop(0, KV_HEADS)
    def _(h):
        for r in backs:

            @pl.when(sends(r))
            def _():
                kv_copy(h, r).wait_send()

            @pl.when(has_prior(r))
            def _():
                grads_copy(h, r).wait_send()

        for active, step, moves in relays:

            @pl.when(active)
            def _():
                for k, (here, there) in enumerate(moves):
                    relay_copy(h, k, step, here, there).wait_send()


def body(queries, keys, values, grad_out, starts, pattern):
    group = queries.shape[1] // keys.shape[1]
    smem = pl.BlockSpec(memory_space=pltpu.SMEM)
    vmem = pl.BlockSpec(memory_space=pltpu.VMEM)
    pair = (KV_HEADS, 2, BLOCK, HEAD_DIM)
    sems = pltpu.SemaphoreType.DMA((BACK, KV_HEADS))
    return pl.pallas_call(
        functools.partial(kernel, group),
        in_specs=[smem, smem] + [vmem] * 4,
        out_specs=[vmem] * 3,
        out_shape=[
            jax.ShapeDtypeStruct(queries.shape, jnp.bfloat16),
            jax.ShapeDtypeStruct(keys.shape, jnp.bfloat16),
            jax.ShapeDtypeStruct(values.shape, jnp.bfloat16),
        ],
        scratch_shapes=[
            pltpu.VMEM(pair, jnp.bfloat16),
            pltpu.VMEM((BACK,) + pair, jnp.bfloat16),
            pltpu.VMEM(pair, jnp.float32),
            pltpu.VMEM((BACK,) + pair, jnp.bfloat16),
            pltpu.VMEM((BACK,) + pair, jnp.bfloat16),
            pltpu.VMEM(((BACK + 1) * BLOCK, BLOCK), jnp.float32),
            sems,
            sems,
            pltpu.SemaphoreType.DMA((2, KV_HEADS)),
            sems,
            sems,
        ],
        compiler_params=pltpu.CompilerParams(
            collective_id=0, has_side_effects=True, vmem_limit_bytes=48 * 2**20
        ),
    )(starts, pattern, queries, grad_out, keys, values)


def solution(mesh):
    rows = P(AXES, None)
    return jax.shard_map(
        body,
        mesh=mesh,
        in_specs=(rows, rows, rows, rows, P(), P()),
        out_specs=(rows, rows, rows),
        check_vma=False,
    )
```

```python
import functools
import math

import jax
import jax.numpy as jnp
from jax import lax
from jax.experimental import pallas as pl
from jax.experimental.pallas import tpu as pltpu
from jax.sharding import PartitionSpec as P

KV_HEADS = 8
HEAD_DIM = 128
WINDOW = 512
BLOCK = 128
BACK = WINDOW // BLOCK
AXES = ("seq", "head")
LEAD = 2

SCALE = 1.0 / math.sqrt(HEAD_DIM)


def mask_bias(first_row, starts_ref, pattern_ref, block):
    shape = ((BACK + 1) * BLOCK, BLOCK)
    row = lax.broadcasted_iota(jnp.int32, shape, 0)
    query_pos = first_row + lax.broadcasted_iota(jnp.int32, shape, 1)
    back = row // BLOCK
    key_pos = first_row - back * BLOCK + (row - back * BLOCK)
    crossed = jnp.zeros(shape, jnp.int32)
    for i in range(starts_ref.shape[0]):
        start = starts_ref[i]
        crossed += ((start <= query_pos) & (start > key_pos)).astype(jnp.int32)
    opened = jnp.zeros(shape, jnp.int32)
    for r in range(BACK + 1):
        opened += jnp.where(back == r, pattern_ref[block, r], 0)
    allowed = (
        (key_pos <= query_pos)
        & (query_pos - key_pos < WINDOW)
        & (key_pos >= 0)
        & (crossed == 0)
        & (opened > 0)
    )
    return jnp.where(allowed, 0.0, -1e30).astype(jnp.float32)


def dot(a, b, dims):
    return lax.dot_general(a, b, (dims, ((), ())), preferred_element_type=jnp.float32)


def head_terms(query_ref, grad_ref, query_grad_ref, first_col, group, key, value, bias):
    key_grad = None
    value_grad = None
    bias = jnp.concatenate([bias, bias], axis=1)
    for pair in range(group // 2):
        cols = [
            pl.ds(pl.multiple_of(first_col + (2 * pair + i) * HEAD_DIM, HEAD_DIM), HEAD_DIM)
            for i in range(2)
        ]
        query = jnp.concatenate([query_ref[:, c] for c in cols], axis=0)
        grad = jnp.concatenate([grad_ref[:, c] for c in cols], axis=0)
        score = dot(key, query, ((1,), (1,))) * (SCALE * math.log2(math.e)) + bias
        expo = jnp.exp2(score - jnp.max(score, axis=0, keepdims=True))
        probs = expo * (1.0 / jnp.sum(expo, axis=0, keepdims=True))
        probs_low = probs.astype(jnp.bfloat16)
        prob_grad = dot(value, grad, ((1,), (1,)))
        row_dot = jnp.sum(probs * prob_grad, axis=0, keepdims=True)
        score_grad = (probs * (prob_grad - row_dot)).astype(jnp.bfloat16)
        value_part = dot(probs_low, grad, ((1,), (0,)))
        key_part = dot(score_grad, query, ((1,), (0,)))
        value_grad = value_part if value_grad is None else value_grad + value_part
        key_grad = key_part if key_grad is None else key_grad + key_part
        query_grad = (dot(score_grad, key, ((0,), (0,))) * SCALE).astype(jnp.bfloat16)
        for i in range(2):
            query_grad_ref[:, cols[i]] = query_grad[i * BLOCK : (i + 1) * BLOCK]
    return key_grad * SCALE, value_grad


def kernel(
    group,
    starts_ref,
    pattern_ref,
    query_ref,
    grad_ref,
    key_ref,
    value_ref,
    query_grad_ref,
    key_grad_ref,
    value_grad_ref,
    own_kv,
    kv_in,
    own_grads,
    grads_out,
    grads_in,
    fold_in,
    bias_ref,
    kv_send,
    kv_recv,
    relay_send,
    grads_send,
    grads_recv,
    fold_recv,
):
    span = lax.axis_size("head")
    devices = lax.axis_size("seq") * span
    block = lax.axis_index("seq") * span + lax.axis_index("head")
    backs = range(1, BACK + 1)

    def place(other):
        return (lax.div(other, span), lax.rem(other, span))

    def has_next(r):
        return block + r < devices

    def has_prior(r):
        return block >= r

    lane = lax.rem(block, BACK)
    direct = {1: lane != 3, 2: (lane == 0) | (lane == 3), 3: lane != 0, 4: lane >= 0}
    upward = lane == 2
    downward = (lane == 1) & (block >= BACK)
    relays = (
        (upward, 1, ((2, 3), (1, 2))),
        (downward, devices - 1, ((3, 2), (2, 1))),
    )
    early = {
        1: upward,
        2: upward | downward,
        3: downward,
        4: lane < 0,
    }

    top = lane == 3
    bottom = (lane == 0) & (block >= BACK)
    leaves = ((top, devices - 1, (3, 2)), (bottom, 1, (2, 1)))
    leaf = {1: bottom, 2: top | bottom, 3: top, 4: lane < 0}

    def sends(r):
        return has_next(r) & direct[r]

    def waits_late(r):
        return has_prior(r) & jnp.logical_not(early[r])

    def kv_copy(h, r):
        return pltpu.make_async_remote_copy(
            src_ref=own_kv.at[h],
            dst_ref=kv_in.at[r - 1, h],
            send_sem=kv_send.at[r - 1, h],
            recv_sem=kv_recv.at[r - 1, h],
            device_id=place(lax.rem(block + r, devices)),
            device_id_type=pl.DeviceIdType.MESH,
        )

    def grads_copy(h, r):
        return pltpu.make_async_remote_copy(
            src_ref=grads_out.at[r - 1, h],
            dst_ref=grads_in.at[r - 1, h],
            send_sem=grads_send.at[r - 1, h],
            recv_sem=grads_recv.at[r - 1, h],
            device_id=place(lax.rem(block + devices - r, devices)),
            device_id_type=pl.DeviceIdType.MESH,
        )

    def relay_copy(h, k, step, here, there):
        return pltpu.make_async_remote_copy(
            src_ref=kv_in.at[here - 1, h],
            dst_ref=kv_in.at[there - 1, h],
            send_sem=relay_send.at[k, h],
            recv_sem=kv_recv.at[there - 1, h],
            device_id=place(lax.rem(block + step, devices)),
            device_id_type=pl.DeviceIdType.MESH,
        )

    def hand_on(h):
        for active, step, moves in relays:

            @pl.when(active)
            def _():
                for k, (here, there) in enumerate(moves):
                    kv_copy(h, here).wait_recv()
                    relay_copy(h, k, step, here, there).start()

    def leaf_copy(h, k, step, here):
        return pltpu.make_async_remote_copy(
            src_ref=grads_out.at[here - 1, h],
            dst_ref=fold_in.at[k, h],
            send_sem=grads_send.at[here - 1, h],
            recv_sem=fold_recv.at[k, h],
            device_id=place(lax.rem(block + step, devices)),
            device_id_type=pl.DeviceIdType.MESH,
        )

    def fold(h):
        for active, step, moves in relays:

            @pl.when(active)
            def _():
                for k, (here, _) in enumerate(moves):
                    leaf_copy(h, k, step, here).wait_recv()
                    grads_out[here - 1, h] = (
                        grads_out[here - 1, h].astype(jnp.float32)
                        + fold_in[k, h].astype(jnp.float32)
                    ).astype(jnp.bfloat16)
                    grads_copy(h, here).start()

    barrier = pltpu.get_barrier_semaphore()
    for r in backs:
        for there, step in ((has_next(r), r), (has_prior(r), devices - r)):

            @pl.when(there)
            def _():
                pl.semaphore_signal(
                    barrier,
                    inc=1,
                    device_id=place(lax.rem(block + step, devices)),
                    device_id_type=pl.DeviceIdType.MESH,
                )

    for h in range(KV_HEADS):
        own_kv[h, 0] = key_ref[:, h * HEAD_DIM : (h + 1) * HEAD_DIM]
        own_kv[h, 1] = value_ref[:, h * HEAD_DIM : (h + 1) * HEAD_DIM]
    partners = jnp.minimum(block, BACK) + jnp.minimum(devices - 1 - block, BACK)
    pl.semaphore_wait(barrier, partners)

    @pl.loop(0, KV_HEADS)
    def _(h):
        for r in backs:

            @pl.when(sends(r))
            def _():
                kv_copy(h, r).start()

    for r in backs:

        @pl.when(jnp.logical_not(has_prior(r)))
        def _():
            kv_in[r - 1] = jnp.zeros(kv_in.shape[1:], kv_in.dtype)

        @pl.when(jnp.logical_not(sends(r)))
        def _():
            grads_in[r - 1] = jnp.zeros(grads_in.shape[1:], grads_in.dtype)

    bias_ref[...] = mask_bias(block * BLOCK, starts_ref, pattern_ref, block)

    for h in range(LEAD):
        hand_on(h)

    @pl.loop(0, KV_HEADS)
    def _(h):
        @pl.when(h + LEAD < KV_HEADS)
        def _():
            hand_on(h + LEAD)

        for r in backs:

            @pl.when(waits_late(r))
            def _():
                kv_copy(h, r).wait_recv()

        key, value = (
            jnp.concatenate([own_kv[h, i]] + [kv_in[r - 1, h, i] for r in backs], axis=0)
            for i in range(2)
        )
        terms = head_terms(
            query_ref,
            grad_ref,
            query_grad_ref,
            h * (group * HEAD_DIM),
            group,
            key,
            value,
            bias_ref[...],
        )
        for i in range(2):
            own_grads[h, i] = terms[i][:BLOCK]
            for r in backs:
                grads_out[r - 1, h, i] = terms[i][r * BLOCK : (r + 1) * BLOCK].astype(
                    jnp.bfloat16
                )
        for r in backs:

            @pl.when(waits_late(r) & jnp.logical_not(leaf[r]))
            def _():
                grads_copy(h, r).start()

        for active, step, sources in leaves:

            @pl.when(active)
            def _():
                for k, here in enumerate(sources):
                    leaf_copy(h, k, step, here).start()

        @pl.when(h >= LEAD)
        def _():
            fold(h - LEAD)

    for h in range(KV_HEADS - LEAD, KV_HEADS):
        fold(h)

    @pl.loop(0, KV_HEADS)
    def _(h):
        for r in backs:

            @pl.when(sends(r))
            def _():
                grads_copy(h, r).wait_recv()

        cols = pl.ds(pl.multiple_of(h * HEAD_DIM, HEAD_DIM), HEAD_DIM)
        for i, out_ref in enumerate((key_grad_ref, value_grad_ref)):
            total = own_grads[h, i]
            for r in backs:
                total += grads_in[r - 1, h, i].astype(jnp.float32)
            out_ref[:, cols] = total.astype(jnp.bfloat16)

    @pl.loop(0, KV_HEADS)
    def _(h):
        for r in backs:

            @pl.when(sends(r))
            def _():
                kv_copy(h, r).wait_send()

            @pl.when(has_prior(r))
            def _():
                grads_copy(h, r).wait_send()

        for active, step, moves in relays:

            @pl.when(active)
            def _():
                for k, (here, there) in enumerate(moves):
                    relay_copy(h, k, step, here, there).wait_send()


def body(queries, keys, values, grad_out, starts, pattern):
    group = queries.shape[1] // keys.shape[1]
    smem = pl.BlockSpec(memory_space=pltpu.SMEM)
    vmem = pl.BlockSpec(memory_space=pltpu.VMEM)
    pair = (KV_HEADS, 2, BLOCK, HEAD_DIM)
    sems = pltpu.SemaphoreType.DMA((BACK, KV_HEADS))
    return pl.pallas_call(
        functools.partial(kernel, group),
        in_specs=[smem, smem] + [vmem] * 4,
        out_specs=[vmem] * 3,
        out_shape=[
            jax.ShapeDtypeStruct(queries.shape, jnp.bfloat16),
            jax.ShapeDtypeStruct(keys.shape, jnp.bfloat16),
            jax.ShapeDtypeStruct(values.shape, jnp.bfloat16),
        ],
        scratch_shapes=[
            pltpu.VMEM(pair, jnp.bfloat16),
            pltpu.VMEM((BACK,) + pair, jnp.bfloat16),
            pltpu.VMEM(pair, jnp.float32),
            pltpu.VMEM((BACK,) + pair, jnp.bfloat16),
            pltpu.VMEM((BACK,) + pair, jnp.bfloat16),
            pltpu.VMEM((2,) + pair, jnp.bfloat16),
            pltpu.VMEM(((BACK + 1) * BLOCK, BLOCK), jnp.float32),
            sems,
            sems,
            pltpu.SemaphoreType.DMA((2, KV_HEADS)),
            sems,
            sems,
            pltpu.SemaphoreType.DMA((2, KV_HEADS)),
        ],
        compiler_params=pltpu.CompilerParams(
            collective_id=0, has_side_effects=True, vmem_limit_bytes=48 * 2**20
        ),
    )(starts, pattern, queries, grad_out, keys, values)


def solution(mesh):
    rows = P(AXES, None)
    return jax.shard_map(
        body,
        mesh=mesh,
        in_specs=(rows, rows, rows, rows, P(), P()),
        out_specs=(rows, rows, rows),
        check_vma=False,
    )
```
